128 devices in a mesh: row: 32 (over z, x_lo, y), col: 4 (over x_hi, core).
Axes of the slice: x: 4 (x_hi: 2, x_lo: 2; x = x_hi * 2 + x_lo), y: 4, z: 4, core: 2. Of those that a mesh axis runs over, the one named last changes fastest.
Arguments:
- features: bfloat16 [32768, 512], P(('col', 'row')), may hold values from -6 to 6
- weight: bfloat16 [512, 512], replicated, may hold values from -0.25 to 0.25
- bias: float32 [512], replicated, may hold values from -3 to 3
- tiles: bfloat16 [32, 4, 64, 256, 256], P('row', 'col'), may hold values from -0.09375 to 0.09375
- tile_rows: int32 [32, 4, 64], P('row', 'col'), may hold values from 0 to 3, as said below
- tile_cols: int32 [32, 4, 64], P('row', 'col'), may hold values from 0 to 31
- tile_count: int32 [32, 4], P('row', 'col'), may hold values from 16 to 64, as said below
- cotangent: bfloat16 [32768, 512], P(('row', 'col')), may hold values from -6 to 6
Outputs:
- activations: bfloat16 [32768, 512], P(('row', 'col'))
- grad_features: bfloat16 [32768, 512], P(('col', 'row'))
- grad_weight: float32 [512, 512], replicated
The draws below stay inside these ranges and needn't reach their ends.
Inputs may be any that keep to these rules, and one draw needn't show every extreme that they name: The 64 slots of one device name distinct (tile_rows, tile_cols) pairs; the live ones are the first tile_count of them. `tile_count`: some device has all 64 slots live in every draw.
All inputs are finite; a program needn't handle non-finite values.
Results may differ from the reference program's by a relative error of at most 0.03.
Values may be sent and summed in bfloat16 or wider, within the bound.
No kernel may reach another device: no remote copies, remote signals or barrier semaphores. Data moves between devices by JAX's collectives and lax.ppermute only.
A program may use at most 128 MiB of HBM per device.

```python
import jax
import jax.numpy as jnp
from jax import lax

F = 512
TB = 256
BLK_DEV = 1
ROW_TILES = 16
SLOTS = 64
NODES = 32768
N_ROW = 32
N_COL = 4


def tile_pairs(key):
    key = jax.random.fold_in(key, 101)
    block_pairs = N_COL * BLK_DEV * N_ROW * BLK_DEV
    keys = jax.random.split(key, N_ROW * N_COL)
    orders = jax.vmap(lambda one_key: jax.random.permutation(one_key, block_pairs))(keys)
    return orders[:, :SLOTS].reshape(N_ROW, N_COL, SLOTS).astype(jnp.int32)


def draw_tile_rows(key, part):
    pairs = tile_pairs(key)
    return (pairs // (N_ROW * BLK_DEV)).astype(jnp.int32)


def draw_tile_cols(key, part):
    pairs = tile_pairs(key)
    return (pairs % (N_ROW * BLK_DEV)).astype(jnp.int32)


def draw_tile_count(key, part):
    key = jax.random.fold_in(key, 7)
    counts = jax.random.randint(key, (N_ROW * N_COL,), SLOTS // 4, SLOTS + 1)
    fullest = jax.random.randint(jax.random.fold_in(key, 1), (), 0, N_ROW * N_COL)
    counts = counts.at[fullest].set(SLOTS)
    return counts.reshape(N_ROW, N_COL).astype(jnp.int32)


def levels(stream_key, extent, shards, smallest, high):
    loudness = 1.0
    for dim, shards_of in shards:
        draws = jax.random.uniform(jax.random.fold_in(jax.random.fold_in(stream_key, 6), dim), (shards_of,), jnp.float32, smallest / len(shards), high / len(shards))
        loudness = loudness * jnp.repeat(jnp.exp(draws), extent[dim] // shards_of).reshape((-1,) + (1,) * (len(extent) - 1 - dim))
    return loudness


def centred(key, shape, scale, bound, cuts=(), kind=jnp.bfloat16):
    loudness = levels(key, shape, cuts, -0.22, 0.18) if cuts else 1.0
    drawn = jax.random.normal(key, shape, jnp.float32) * scale * loudness
    return jnp.minimum(jnp.maximum(drawn, -bound), bound).astype(kind)


def setup_inputs(seed: int = 0) -> dict:
    seeds = jax.random.split(jax.random.key(seed), 9)
    features = centred(seeds[0], (NODES, F), 1.0, 6.0, ((0, 128),))
    weight = centred(seeds[1], (F, F), F ** -0.5, 0.25)
    bias = centred(seeds[2], (F,), 0.5, 3.0, (), jnp.float32)
    tiles = centred(seeds[3], (N_ROW, N_COL, SLOTS, TB, TB), (ROW_TILES * TB) ** -0.5, 0.09375, ((0, 32), (1, 4)))
    tile_rows = draw_tile_rows(jax.random.fold_in(seeds[8], 71), 0)
    tile_cols = draw_tile_cols(jax.random.fold_in(seeds[8], 71), 0)
    tile_count = draw_tile_count(jax.random.fold_in(seeds[8], 71), 0)
    cotangent = centred(seeds[7], (NODES, F), 1.0, 6.0, ((0, 128),))
    return {"features": features, "weight": weight, "bias": bias, "tiles": tiles, "tile_rows": tile_rows, "tile_cols": tile_cols, "tile_count": tile_count, "cotangent": cotangent}


def reference(features, weight, bias, tiles, tile_rows, tile_cols, tile_count, cotangent):
    row_blocks = N_COL * BLK_DEV
    col_blocks = N_ROW * BLK_DEV
    projected = jnp.dot(features, weight, preferred_element_type=jnp.float32).astype(jnp.bfloat16)
    proj_blocks = projected.reshape(N_COL, col_blocks, TB, F)
    slot_ids = jnp.arange(SLOTS, dtype=jnp.int32)
    live = (slot_ids[None, None, :] < tile_count[:, :, None]).astype(jnp.float32)
    col_range = jnp.arange(N_COL, dtype=jnp.int32)[:, None]

    def forward_rows(rindex):
        picked = proj_blocks[col_range, tile_cols[rindex]]
        prods = jnp.einsum('csij,csjf->csif', tiles[rindex].astype(jnp.float32), picked.astype(jnp.float32))
        prods = prods * live[rindex][:, :, None, None]
        onehot = (tile_rows[rindex][:, :, None] == jnp.arange(row_blocks, dtype=jnp.int32)[None, None, :]).astype(jnp.float32)
        return jnp.einsum('csk,csif->kif', onehot, prods, precision=lax.Precision.HIGHEST)

    pre = lax.map(forward_rows, jnp.arange(N_ROW, dtype=jnp.int32)).reshape(NODES, F)
    shifted = pre + bias[None, :]
    activations = jax.nn.silu(shifted).astype(jnp.bfloat16)
    sig = jax.nn.sigmoid(shifted)
    slope = sig * (1.0 + shifted * (1.0 - sig))
    grad_pre = (cotangent.astype(jnp.float32) * slope).astype(jnp.bfloat16)
    grad_blocks = grad_pre.reshape(N_ROW, row_blocks, TB, F)

    def backward_rows(total, rindex):
        picked = grad_blocks[rindex][tile_rows[rindex]]
        prods = jnp.einsum('csji,csjf->csif', tiles[rindex].astype(jnp.float32), picked.astype(jnp.float32))
        prods = prods * live[rindex][:, :, None, None]
        targets = (col_range * col_blocks + tile_cols[rindex]).reshape(-1)
        part = jax.ops.segment_sum(prods.reshape(N_COL * SLOTS, TB, F), targets, num_segments=N_COL * col_blocks)
        rounded = lax.optimization_barrier(part.astype(jnp.bfloat16))
        return total + rounded.astype(jnp.float32), None

    start = jnp.zeros((N_COL * col_blocks, TB, F), jnp.float32)
    summed, _ = lax.scan(backward_rows, start, jnp.arange(N_ROW, dtype=jnp.int32))
    grad_t = summed.reshape(NODES, F).astype(jnp.bfloat16)
    grad_weight = jnp.dot(features.T, grad_t, preferred_element_type=jnp.float32) * (NODES ** -0.5)
    grad_features = jnp.dot(grad_t, weight.T, preferred_element_type=jnp.float32).astype(jnp.bfloat16)
    return activations, grad_features, grad_weight
```

```python
import functools

import jax
import jax.numpy as jnp
from jax import lax
from jax.experimental import pallas as pl
from jax.experimental.pallas import tpu as pltpu
from jax.sharding import PartitionSpec as P

BF = jnp.bfloat16
F32 = jnp.float32
Z, XL, Y, XH, CORE = 4, 2, 4, 2, 2


def from_row(value, dz=0, dx=0, dy=0):
    pairs = []
    for z in range(Z):
        for x in range(XL):
            for y in range(Y):
                source = (((z + dz) % Z) * XL + (x + dx) % XL) * Y + (y + dy) % Y
                pairs.append((source, (z * XL + x) * Y + y))
    return lax.ppermute(value, "row", pairs)


def from_col(value, dh=0, dc=0):
    pairs = []
    for h in range(XH):
        for c in range(CORE):
            pairs.append((((h + dh) % XH) * CORE + (c + dc) % CORE, h * CORE + c))
    return lax.ppermute(value, "col", pairs)


def along(axis):
    if axis == "y":
        return lambda value, d: from_row(value, dy=d)
    return lambda value, d: from_row(value, dz=d)


def gather_ring(own, first, second):
    get1, get2 = along(first), along(second)
    line = jnp.concatenate([own, get1(own, 1), get1(own, 2), get1(own, 3)])
    half = line.shape[0] // 2
    low, high = line[:half], line[half:]
    near_low = get2(low, 1)
    back_high = get2(high, -1)
    near_high = get2(high, 1)
    back_low = get2(low, -1)
    far_low = get2(near_low, 1)
    far_high = get2(back_high, -1)
    return [low, high, near_low, near_high, far_low, far_high, back_low, back_high]


def scatter_ring(parts, first, second):
    get1, get2 = along(first), along(second)
    low, high, near_low, near_high, far_low, far_high, back_low, back_high = parts
    pass_low = get2(far_low, -1)
    pass_high = get2(far_high, 1)
    got_near_high = get2(near_high, -1)
    got_back_low = get2(back_low, 1)
    sum_near_low = (near_low.astype(F32) + pass_low.astype(F32)).astype(BF)
    sum_back_high = (back_high.astype(F32) + pass_high.astype(F32)).astype(BF)
    got_near_low = get2(sum_near_low, -1)
    got_back_high = get2(sum_back_high, 1)
    low = low.astype(F32) + got_near_low.astype(F32) + got_back_low.astype(F32)
    high = high.astype(F32) + got_near_high.astype(F32) + got_back_high.astype(F32)
    line = jnp.concatenate([low, high]).astype(BF)
    q = line.shape[0] // 4
    total = line[:q].astype(F32)
    for d in (1, 2, 3):
        total = total + get1(line[d * q : (d + 1) * q], -d).astype(F32)
    return total


def dense_kernel(table, tiles, near, far, zeros, sems):
    width = tiles.shape[-1] // 2
    cols = near.shape[1] // width

    for half, dense in enumerate((near, far)):

        def place(p, carry, half=half, dense=dense):
            slot = table[half * 64 + p]
            rows = pl.ds(pl.multiple_of((p // 16) * 256, 256), 256)
            dz = (p // 4) % 4
            dy = p % 4
            col_a = pl.multiple_of((dz * 4 + dy) * width, width)
            col_b = pl.multiple_of((cols // 2 + dy * 4 + dz) * width, width)
            dst_a = dense.at[rows, pl.ds(col_a, width)]
            dst_b = dense.at[rows, pl.ds(col_b, width)]

            @pl.when(slot >= 0)
            def _():
                pltpu.make_async_copy(tiles.at[slot, :, pl.ds(0, width)], dst_a, sems.at[half]).start()
                pltpu.make_async_copy(tiles.at[slot, :, pl.ds(width, width)], dst_b, sems.at[half]).start()

            @pl.when(slot < 0)
            def _():
                pltpu.make_async_copy(zeros, dst_a, sems.at[half]).start()
                pltpu.make_async_copy(zeros, dst_b, sems.at[half]).start()

            return carry

        if half == 0:
            zeros[...] = jnp.zeros_like(zeros)
        lax.fori_loop(0, 64, place, 0)
    pltpu.make_async_copy(near, near, sems.at[0]).wait()
    pltpu.make_async_copy(far, far, sems.at[1]).wait()


def make_dense(table, tiles):
    tile = tiles.shape[-1]
    shape = jax.ShapeDtypeStruct((4 * tile, 16 * tile), BF)
    return pl.pallas_call(
        dense_kernel,
        out_shape=(shape, shape),
        in_specs=[
            pl.BlockSpec(memory_space=pltpu.SMEM),
            pl.BlockSpec(memory_space=pl.ANY),
        ],
        out_specs=(pl.BlockSpec(memory_space=pl.ANY),) * 2,
        scratch_shapes=[
            pltpu.VMEM((tile, tile // 2), BF),
            pltpu.SemaphoreType.DMA((2,)),
        ],
        cost_estimate=pl.CostEstimate(flops=0, bytes_accessed=24 << 20, transcendentals=0),
    )(table, tiles)


def all_sum(term, z, y, core):
    rows = term.shape[0]

    def scatter(value, get, me):
        q = value.shape[0] // 4
        value = value.astype(BF)
        total = lax.dynamic_slice_in_dim(value, me * q, q).astype(F32)
        for d in (1, 2, 3):
            piece = lax.dynamic_slice_in_dim(value, ((me + d) % 4) * q, q)
            total = total + get(piece, -d).astype(F32)
        return total

    def gather(value, get, me):
        q = value.shape[0]
        ring = [value] + [get(value, d) for d in (1, 2, 3)]
        return lax.dynamic_slice_in_dim(jnp.concatenate(ring + ring[:3]), ((4 - me) % 4) * q, 4 * q)

    half = rows // 2
    term = term.astype(BF)
    mine = lax.dynamic_slice_in_dim(term, core * half, half)
    other = lax.dynamic_slice_in_dim(term, (1 - core) * half, half)
    value = mine.astype(F32) + from_col(other, dc=1).astype(F32)
    value = scatter(value, along("y"), y)
    value = scatter(value, along("z"), z).astype(BF)
    value = (value.astype(F32) + from_row(value, dx=1).astype(F32)).astype(BF)
    value = (value.astype(F32) + from_col(value, dh=1).astype(F32)).astype(BF)
    value = gather(value, along("z"), z)
    value = gather(value, along("y"), y)
    other = from_col(value, dc=1)
    return jnp.where(core == 0, jnp.concatenate([value, other]), jnp.concatenate([other, value])).astype(F32)


def on_device(features, weight, bias, tiles, tile_rows, tile_cols, tile_count, cotangent):
    nodes, width = features.shape
    tile = tiles.shape[-1]
    slots = tiles.shape[2]
    row, col = lax.axis_index("row"), lax.axis_index("col")
    z, xl, y = row // 8, (row // 4) % 2, row % 4
    xh, core = col // 2, col % 2

    rows, cols = tile_rows.reshape(slots), tile_cols.reshape(slots)
    place_row = ((rows % 2) ^ core) * 2 + ((rows // 2) ^ xh)
    place_col = ((cols // 8 - z) % 4) * 4 + (cols % 4 - y) % 4
    place = (((cols // 4) % 2) ^ xl) * 64 + place_row * 16 + place_col
    ids = jnp.arange(slots, dtype=jnp.int32)
    place = jnp.where(ids < tile_count.reshape(()), place, -1)
    hit = place[None, :] == jnp.arange(128, dtype=jnp.int32)[:, None]
    table = jnp.max(jnp.where(hit, ids[None, :], -1), axis=1)
    dense = make_dense(table, tiles.reshape(slots, tile, tile))

    half = nodes // 2
    other = from_row(features, dx=1)
    partial_rows = None
    for own, matrix in ((features, dense[0]), (other, dense[1])):
        parts = gather_ring(own[:half], "y", "z") + gather_ring(own[half:], "z", "y")
        term = jnp.dot(matrix, jnp.concatenate(parts), preferred_element_type=F32)
        partial_rows = term if partial_rows is None else partial_rows + term
    partial_rows = partial_rows.astype(BF)

    pair = partial_rows[: 2 * nodes].astype(F32) + from_col(partial_rows[2 * nodes :], dc=1).astype(F32)
    aggregate = pair[:nodes] + from_col(pair[nodes:].astype(BF), dh=1).astype(F32)
    aggregate = aggregate.astype(BF)

    shifted = jnp.dot(aggregate, weight, preferred_element_type=F32) + bias[None, :]
    activations = jax.nn.silu(shifted).astype(BF)
    sig = jax.nn.sigmoid(shifted)
    slope = sig * (1.0 + shifted * (1.0 - sig))
    grad_pre = (cotangent.astype(F32) * slope).astype(BF)
    back = lax.dot_general(grad_pre, weight, (((1,), (1,)), ((), ())), preferred_element_type=F32).astype(BF)

    back = jnp.concatenate([back, from_col(back, dh=1)])
    back = jnp.concatenate([back, from_col(back, dc=1)])

    local_weight = lax.dot_general(aggregate, grad_pre, (((0,), (0,)), ((), ())), preferred_element_type=F32)
    node_total = nodes * lax.axis_size("row") * lax.axis_size("col")
    grad_weight = all_sum(local_weight, z, y, core) * node_total ** (-0.5)

    sums = []
    for matrix in (dense[1], dense[0]):
        partial_t = lax.dot_general(matrix, back, (((0,), (0,)), ((), ())), preferred_element_type=F32).astype(BF)
        n = partial_t.shape[0] // 2
        halves = []
        for k, (first, second) in enumerate((("y", "z"), ("z", "y"))):
            parts = [partial_t[k * n + i * n // 8 : k * n + (i + 1) * n // 8] for i in range(8)]
            halves.append(scatter_ring(parts, first, second))
        sums.append(jnp.concatenate(halves))
    grad_features = (sums[1] + from_row(sums[0].astype(BF), dx=1).astype(F32)).astype(BF)
    return (activations, grad_features, grad_weight)


def solution(mesh):
    placed = (
        P(("col", "row"), None),
        P(),
        P(),
        P("row", "col", None, None, None),
        P("row", "col", None),
        P("row", "col", None),
        P("row", "col"),
        P(("row", "col"), None),
    )
    return jax.shard_map(
        on_device,
        mesh=mesh,
        in_specs=placed,
        out_specs=(P(("row", "col"), None), P(("col", "row"), None), P()),
        check_vma=False,
    )
```

```python
import jax
import jax.numpy as jnp
from jax import lax
from jax.experimental import pallas as pl
from jax.experimental.pallas import tpu as pltpu
from jax.sharding import PartitionSpec as P

BF = jnp.bfloat16
F32 = jnp.float32
XL = 4
CHAINS = ((0, 0, (1, 3, 8, 24)), (0, 1, (8, 24, 1, 3)), (1, 0, (3, 1, 24, 8)), (1, 1, (24, 8, 3, 1)))
CORE, XH = 1, 2


def swap(value, axis, mask):
    size = lax.axis_size(axis)
    return lax.ppermute(value, axis, [(i ^ mask, i) for i in range(size)])


def order_of(masks):
    order = [0]
    for mask in masks:
        order = order + [offset ^ mask for offset in order]
    return order


def dense_kernel(table, tiles, *refs):
    outs, (held, sems) = refs[:8], refs[8:]
    step = pl.program_id(0)
    tile = held.shape[-1]
    wide = tile // 2

    @pl.when(step == 0)
    def _():
        def start(slot, carry):
            pltpu.make_async_copy(tiles.at[slot], held.at[slot], sems.at[slot]).start()
            return carry

        lax.fori_loop(0, table[128], start, 0)

    for chain, (plane, half, masks) in enumerate(CHAINS):
        if half:
            continue
        for offset in order_of(masks):
            slot = table[step * 32 + (offset ^ (plane * XL))]
            spots = []
            for part in range(2):
                k = order_of(CHAINS[chain + part][2]).index(offset)
                spots.append((outs[2 * (chain + part) + k // 8], pl.ds((k % 8) * wide, wide)))

            @pl.when(slot >= 0)
            def _(slot=slot, spots=spots):
                pltpu.make_async_copy(tiles.at[slot], held.at[slot], sems.at[slot]).wait()
                for part, (out, lanes) in enumerate(spots):
                    out[:, lanes] = held[slot, :, part * wide : (part + 1) * wide]

            @pl.when(slot < 0)
            def _(spots=spots):
                for out, lanes in spots:
                    out[:, lanes] = jnp.zeros((tile, wide), out.dtype)


def make_dense(table, tiles):
    slots, tile, _ = tiles.shape
    return pl.pallas_call(
        dense_kernel,
        grid=(4,),
        out_shape=(jax.ShapeDtypeStruct((4 * tile, 4 * tile), BF),) * 8,
        in_specs=[
            pl.BlockSpec(memory_space=pltpu.SMEM),
            pl.BlockSpec(memory_space=pl.ANY),
        ],
        out_specs=(pl.BlockSpec((tile, 4 * tile), lambda i: (i, 0)),) * 8,
        scratch_shapes=[pltpu.VMEM((slots, tile, tile), BF), pltpu.SemaphoreType.DMA((slots,))],
        compiler_params=pltpu.CompilerParams(vmem_limit_bytes=24 << 20),
        cost_estimate=pl.CostEstimate(flops=0, bytes_accessed=24 << 20, transcendentals=0),
    )(table, tiles)


def all_sum(term, row, col):
    def scatter(value, me, masks):
        q = value.shape[0] // 4
        value = value.astype(BF)
        total = lax.dynamic_slice_in_dim(value, me * q, q).astype(F32)
        for d, mask in enumerate(masks, 1):
            piece = lax.dynamic_slice_in_dim(value, (me ^ d) * q, q)
            total = total + swap(piece, "row", mask).astype(F32)
        return total

    def gather(value, me, masks):
        pieces = [value] + [swap(value, "row", mask) for mask in masks]
        stacked = jnp.stack(pieces)
        return jnp.concatenate([lax.dynamic_index_in_dim(stacked, me ^ i, keepdims=False) for i in range(4)])

    y, z, core = row % 4, row // 8, col % 2
    half = term.shape[0] // 2
    term = term.astype(BF)
    mine = lax.dynamic_slice_in_dim(term, core * half, half)
    other = lax.dynamic_slice_in_dim(term, (1 - core) * half, half)
    value = mine.astype(F32) + swap(other, "col", CORE).astype(F32)
    value = scatter(value, y, (1, 2, 3))
    value = scatter(value, z, (8, 16, 24)).astype(BF)
    value = (value.astype(F32) + swap(value, "row", XL).astype(F32)).astype(BF)
    value = (value.astype(F32) + swap(value, "col", XH).astype(F32)).astype(BF)
    value = gather(value, z, (8, 16, 24))
    value = gather(value, y, (1, 2, 3))
    other = swap(value, "col", CORE)
    return jnp.where(core == 0, jnp.concatenate([value, other]), jnp.concatenate([other, value])).astype(F32)


def on_device(features, weight, bias, tiles, tile_rows, tile_cols, tile_count, cotangent):
    nodes, width = features.shape
    tile = tiles.shape[-1]
    slots = tiles.shape[2]
    row, col = lax.axis_index("row"), lax.axis_index("col")

    rows, cols = tile_rows.reshape(slots) ^ col, tile_cols.reshape(slots) ^ row
    count = tile_count.reshape(1)
    ids = jnp.arange(slots, dtype=jnp.int32)
    place = ((rows % 2) * 2 + rows // 2) * 32 + cols
    hit = (place[None, :] == jnp.arange(128, dtype=jnp.int32)[:, None]) & (ids < count)[None, :]
    table = jnp.concatenate([jnp.max(jnp.where(hit, ids[None, :], -1), axis=1), count])
    dense = make_dense(table, tiles.reshape(slots, tile, tile))

    half = nodes // 2
    planes = (features, swap(features, "row", XL))
    held = [[planes[plane][part * half : (part + 1) * half]] for plane, part, _ in CHAINS]
    for step in range(4):
        for chain, (_, _, masks) in enumerate(CHAINS):
            so_far = held[chain][0] if step == 0 else jnp.concatenate(held[chain])
            held[chain] = [so_far, swap(so_far, "row", masks[step])]
    aggregate = 0.0
    for part in range(2):
        for chain in range(4):
            aggregate = aggregate + jnp.dot(
                dense[2 * chain + part], held[chain][part], preferred_element_type=F32
            )
    aggregate = aggregate.astype(BF)

    pair = aggregate[: 2 * nodes].astype(F32) + swap(aggregate[2 * nodes :], "col", CORE).astype(F32)
    aggregate = pair[:nodes] + swap(pair[nodes:].astype(BF), "col", XH).astype(F32)
    aggregate = aggregate.astype(BF)

    shifted = jnp.dot(aggregate, weight, preferred_element_type=F32) + bias[None, :]
    activations = jax.nn.silu(shifted).astype(BF)
    sig = jax.nn.sigmoid(shifted)
    slope = sig * (1.0 + shifted * (1.0 - sig))
    grad_pre = (cotangent.astype(F32) * slope).astype(BF)
    back = lax.dot_general(grad_pre, weight, (((1,), (1,)), ((), ())), preferred_element_type=F32).astype(BF)

    back = jnp.concatenate([back, swap(back, "col", XH)])
    back = jnp.concatenate([back, swap(back, "col", CORE)])

    local_weight = lax.dot_general(aggregate, grad_pre, (((0,), (0,)), ((), ())), preferred_element_type=F32)
    node_total = nodes * lax.axis_size("row") * lax.axis_size("col")
    grad_weight = all_sum(local_weight, row, col) * node_total ** (-0.5)

    def product(matrix):
        return lax.dot_general(matrix, back, (((0,), (0,)), ((), ())), preferred_element_type=F32).astype(BF)

    turn = (2, 3, 0, 1)
    far = {chain: product(dense[2 * chain + 1]) for chain in turn}
    got = {chain: swap(far[chain], "row", CHAINS[chain][2][3]) for chain in turn}
    near = {chain: product(dense[2 * chain]) for chain in turn}
    for step in (2, 1, 0):
        for chain in turn:
            n = near[chain].shape[0] // 2
            send = (near[chain][n:].astype(F32) + got[chain][n:].astype(F32)).astype(BF)
            keep = near[chain][:n].astype(F32) + got[chain][:n].astype(F32)
            near[chain] = keep.astype(BF) if step else keep
            got[chain] = swap(send, "row", CHAINS[chain][2][step])
    sums = {chain: near[chain] + got[chain].astype(F32) for chain in turn}
    other = jnp.concatenate([sums[2], sums[3]]).astype(BF)
    own = jnp.concatenate([sums[0], sums[1]])
    grad_features = (own + swap(other, "row", XL).astype(F32)).astype(BF)
    return (activations, grad_features, grad_weight)


def solution(mesh):
    placed = (
        P(("col", "row"), None),
        P(),
        P(),
        P("row", "col", None, None, None),
        P("row", "col", None),
        P("row", "col", None),
        P("row", "col"),
        P(("row", "col"), None),
    )
    return jax.shard_map(
        on_device,
        mesh=mesh,
        in_specs=placed,
        out_specs=(P(("row", "col"), None), P(("col", "row"), None), P()),
        check_vma=False,
    )
```

```python
import jax
import jax.numpy as jnp
from jax import lax
from jax.experimental import pallas as pl
from jax.experimental.pallas import tpu as pltpu
from jax.sharding import PartitionSpec as P

BF = jnp.bfloat16
F32 = jnp.float32
XL = 4
CHAINS = ((0, 0, (1, 3, 8, 24)), (0, 1, (8, 24, 1, 3)), (1, 0, (3, 1, 24, 8)), (1, 1, (24, 8, 3, 1)))
CORE, XH = 1, 2


def swap(value, axis, mask):
    size = lax.axis_size(axis)
    return lax.ppermute(value, axis, [(i ^ mask, i) for i in range(size)])


def order_of(masks):
    order = [0]
    for mask in masks:
        order = order + [offset ^ mask for offset in order]
    return order


def dense_kernel(table, tiles, *refs):
    outs, (held, sems) = refs[-10:-2], refs[-2:]
    step = pl.program_id(0)
    tile = held.shape[-1]
    wide = tile // 2

    @pl.when(step == 0)
    def _():
        def start(slot, carry):
            pltpu.make_async_copy(tiles.at[slot], held.at[slot], sems.at[slot]).start()
            return carry

        lax.fori_loop(0, table[128], start, 0)

    for chain, (plane, half, masks) in enumerate(CHAINS):
        if half:
            continue
        for offset in order_of(masks):
            slot = table[step * 32 + (offset ^ (plane * XL))]
            spots = []
            for part in range(2):
                k = order_of(CHAINS[chain + part][2]).index(offset)
                spots.append((outs[2 * (chain + part) + k // 8], pl.ds((k % 8) * wide, wide)))

            @pl.when(slot >= 0)
            def _(slot=slot, spots=spots):
                pltpu.make_async_copy(tiles.at[slot], held.at[slot], sems.at[slot]).wait()
                for part, (out, lanes) in enumerate(spots):
                    out[:, lanes] = held[slot, :, part * wide : (part + 1) * wide]

            @pl.when(slot < 0)
            def _(spots=spots):
                for out, lanes in spots:
                    out[:, lanes] = jnp.zeros((tile, wide), out.dtype)


def make_dense(table, tiles, *after):
    slots, tile, _ = tiles.shape
    return pl.pallas_call(
        dense_kernel,
        grid=(4,),
        out_shape=(jax.ShapeDtypeStruct((4 * tile, 4 * tile), BF),) * 8,
        in_specs=[
            pl.BlockSpec(memory_space=pltpu.SMEM),
            pl.BlockSpec(memory_space=pl.ANY),
        ]
        + [pl.BlockSpec(memory_space=pl.ANY)] * len(after),
        out_specs=(pl.BlockSpec((tile, 4 * tile), lambda i: (i, 0)),) * 8,
        scratch_shapes=[pltpu.VMEM((slots, tile, tile), BF), pltpu.SemaphoreType.DMA((slots,))],
        compiler_params=pltpu.CompilerParams(vmem_limit_bytes=24 << 20),
        cost_estimate=pl.CostEstimate(flops=0, bytes_accessed=24 << 20, transcendentals=0),
    )(table, tiles, *after)


def zero_of(value):
    return value[0, 0].astype(F32) * 0.0


def plane_groups():
    return [[z * 8 + x * 4 + y for z in range(4) for y in range(4)] for x in range(2)]


def sum_pieces(term, col):
    half = term.shape[0] // 2
    core = col % 2
    term = term.astype(BF)
    mine = lax.dynamic_slice_in_dim(term, core * half, half)
    other = lax.dynamic_slice_in_dim(term, (1 - core) * half, half)
    value = (mine.astype(F32) + swap(other, "col", CORE).astype(F32)).astype(BF)
    value = lax.all_to_all(value, "row", 0, 0, axis_index_groups=plane_groups(), tiled=True)
    return jnp.sum(value.reshape(16, half // 16, -1).astype(F32), axis=0)


def sum_rest(value):
    value = value.astype(BF)
    value = (value.astype(F32) + swap(value, "row", XL).astype(F32)).astype(BF)
    return (value.astype(F32) + swap(value, "col", XH).astype(F32)).astype(BF)


def spread(value, col):
    value = lax.all_gather(value, "row", axis_index_groups=plane_groups(), axis=0, tiled=True)
    other = swap(value, "col", CORE)
    first = col % 2 == 0
    return jnp.concatenate([jnp.where(first, value, other), jnp.where(first, other, value)]).astype(F32)


def on_device(features, weight, bias, tiles, tile_rows, tile_cols, tile_count, cotangent):
    nodes, width = features.shape
    tile = tiles.shape[-1]
    slots = tiles.shape[2]
    row, col = lax.axis_index("row"), lax.axis_index("col")

    rows, cols = tile_rows.reshape(slots) ^ col, tile_cols.reshape(slots) ^ row
    count = tile_count.reshape(1)
    ids = jnp.arange(slots, dtype=jnp.int32)
    place = ((rows % 2) * 2 + rows // 2) * 32 + cols
    hit = (place[None, :] == jnp.arange(128, dtype=jnp.int32)[:, None]) & (ids < count)[None, :]
    table = jnp.concatenate([jnp.max(jnp.where(hit, ids[None, :], -1), axis=1), count])

    half = nodes // 2
    planes = (features, swap(features, "row", XL))
    held = [[planes[plane][part * half : (part + 1) * half]] for plane, part, _ in CHAINS]
    for step in range(4):
        for chain, (_, _, masks) in enumerate(CHAINS):
            so_far = held[chain][0] if step == 0 else jnp.concatenate(held[chain])
            held[chain] = [so_far, swap(so_far, "row", masks[step])]
        if step == 2:
            dense = make_dense(table, tiles.reshape(slots, tile, tile), *[parts[1] for parts in held])
    aggregate = 0.0
    for part in range(2):
        for chain in range(4):
            aggregate = aggregate + jnp.dot(
                dense[2 * chain + part], held[chain][part], preferred_element_type=F32
            )
    aggregate = aggregate.astype(BF)

    pair = aggregate[: 2 * nodes].astype(F32) + swap(aggregate[2 * nodes :], "col", CORE).astype(F32)
    aggregate = pair[:nodes] + swap(pair[nodes:].astype(BF), "col", XH).astype(F32)
    aggregate = aggregate.astype(BF)

    shifted = jnp.dot(aggregate, weight, preferred_element_type=F32) + bias[None, :]
    activations = jax.nn.silu(shifted).astype(BF)
    sig = jax.nn.sigmoid(shifted)
    slope = sig * (1.0 + shifted * (1.0 - sig))
    grad_pre = (cotangent.astype(F32) * slope).astype(BF)
    back = lax.dot_general(weight, grad_pre, (((1,), (1,)), ((), ())), preferred_element_type=F32).astype(BF)

    back = jnp.concatenate([back, swap(back, "col", XH)], axis=1)
    back = jnp.concatenate([back, swap(back, "col", CORE)], axis=1)

    local_weight = lax.dot_general(aggregate, grad_pre, (((0,), (0,)), ((), ())), preferred_element_type=F32)

    def product(matrix):
        return jnp.dot(back, matrix, preferred_element_type=F32).astype(BF)

    turn = (2, 3, 0, 1)
    far = {chain: product(dense[2 * chain + 1]) for chain in turn}
    got = {chain: swap(far[chain], "row", CHAINS[chain][2][3]) for chain in turn}
    near = {chain: product(dense[2 * chain]) for chain in turn}
    piece = sum_pieces(local_weight + zero_of(far[1]), col)
    tie = zero_of(piece)
    for step in (2, 1, 0):
        if step == 1:
            piece = sum_rest(piece)
            tie = zero_of(piece)
        for chain in turn:
            n = near[chain].shape[1] // 2
            send = (near[chain][:, n:].astype(F32) + got[chain][:, n:].astype(F32) + tie).astype(BF)
            keep = near[chain][:, :n].astype(F32) + got[chain][:, :n].astype(F32)
            near[chain] = keep.astype(BF) if step else keep
            got[chain] = swap(send, "row", CHAINS[chain][2][step])
    node_total = nodes * lax.axis_size("row") * lax.axis_size("col")
    grad_weight = spread(piece, col) * node_total ** (-0.5)
    sums = {chain: near[chain] + got[chain].astype(F32) for chain in turn}
    other = jnp.concatenate([sums[2], sums[3]], axis=1).astype(BF)
    own = jnp.concatenate([sums[0], sums[1]], axis=1)
    grad_features = (own + swap(other, "row", XL).astype(F32)).astype(BF).T
    return (activations, grad_features, grad_weight)


def solution(mesh):
    placed = (
        P(("col", "row"), None),
        P(),
        P(),
        P("row", "col", None, None, None),
        P("row", "col", None),
        P("row", "col", None),
        P("row", "col"),
        P(("row", "col"), None),
    )
    return jax.shard_map(
        on_device,
        mesh=mesh,
        in_specs=placed,
        out_specs=(P(("row", "col"), None), P(("col", "row"), None), P()),
        check_vma=False,
    )
```

```python
import jax
import jax.numpy as jnp
from jax import lax
from jax.experimental import pallas as pl
from jax.experimental.pallas import tpu as pltpu
from jax.sharding import PartitionSpec as P

BF = jnp.bfloat16
F32 = jnp.float32
XL = 4
CHAINS = ((0, 0, (1, 3, 8, 24)), (0, 1, (8, 24, 1, 3)), (1, 0, (3, 1, 24, 8)), (1, 1, (24, 8, 3, 1)))
CORE, XH = 1, 2


def swap(value, axis, mask):
    size = lax.axis_size(axis)
    return lax.ppermute(value, axis, [(i ^ mask, i) for i in range(size)])


def order_of(masks):
    order = [0]
    for mask in masks:
        order = order + [offset ^ mask for offset in order]
    return order


def dense_kernel(table, tiles, *refs):
    outs, (held, sems) = refs[-10:-2], refs[-2:]
    step = pl.program_id(0)
    tile = held.shape[-1]
    wide = tile // 2

    @pl.when(step == 0)
    def _():
        def start(slot, carry):
            pltpu.make_async_copy(tiles.at[slot], held.at[slot], sems.at[slot]).start()
            return carry

        lax.fori_loop(0, table[128], start, 0)

    for chain, (plane, half, masks) in enumerate(CHAINS):
        if half:
            continue
        for offset in order_of(masks):
            slot = table[step * 32 + (offset ^ (plane * XL))]
            spots = []
            for part in range(2):
                k = order_of(CHAINS[chain + part][2]).index(offset)
                spots.append((outs[2 * (chain + part) + k // 8], pl.ds((k % 8) * wide, wide)))

            @pl.when(slot >= 0)
            def _(slot=slot, spots=spots):
                pltpu.make_async_copy(tiles.at[slot], held.at[slot], sems.at[slot]).wait()
                for part, (out, lanes) in enumerate(spots):
                    out[:, lanes] = held[slot, :, part * wide : (part + 1) * wide]

            @pl.when(slot < 0)
            def _(spots=spots):
                for out, lanes in spots:
                    out[:, lanes] = jnp.zeros((tile, wide), out.dtype)


def make_dense(table, tiles, *after):
    slots, tile, _ = tiles.shape
    return pl.pallas_call(
        dense_kernel,
        grid=(4,),
        out_shape=(jax.ShapeDtypeStruct((4 * tile, 4 * tile), BF),) * 8,
        in_specs=[
            pl.BlockSpec(memory_space=pltpu.SMEM),
            pl.BlockSpec(memory_space=pl.ANY),
        ]
        + [pl.BlockSpec(memory_space=pl.ANY)] * len(after),
        out_specs=(pl.BlockSpec((tile, 4 * tile), lambda i: (i, 0)),) * 8,
        scratch_shapes=[pltpu.VMEM((slots, tile, tile), BF), pltpu.SemaphoreType.DMA((slots,))],
        compiler_params=pltpu.CompilerParams(vmem_limit_bytes=24 << 20),
        cost_estimate=pl.CostEstimate(flops=0, bytes_accessed=24 << 20, transcendentals=0),
    )(table, tiles, *after)


def zero_of(value):
    return value[0, 0].astype(F32) * 0.0


def halve(value, axis, mask):
    half = value.shape[0] // 2
    bit = ((lax.axis_index(axis) & mask) != 0).astype(jnp.int32)
    value = value.astype(BF)
    mine = lax.dynamic_slice_in_dim(value, bit * half, half)
    other = lax.dynamic_slice_in_dim(value, (1 - bit) * half, half)
    return mine.astype(F32) + swap(other, axis, mask).astype(F32)


def both(value, axis, mask):
    value = value.astype(BF)
    return value.astype(F32) + swap(value, axis, mask).astype(F32)


def spread(value, axis, mask):
    value = value.astype(BF)
    other = swap(value, axis, mask)
    first = (lax.axis_index(axis) & mask) == 0
    return jnp.concatenate([jnp.where(first, value, other), jnp.where(first, other, value)])


def on_device(features, weight, bias, tiles, tile_rows, tile_cols, tile_count, cotangent):
    nodes, width = features.shape
    tile = tiles.shape[-1]
    slots = tiles.shape[2]
    row, col = lax.axis_index("row"), lax.axis_index("col")

    rows, cols = tile_rows.reshape(slots) ^ col, tile_cols.reshape(slots) ^ row
    count = tile_count.reshape(1)
    ids = jnp.arange(slots, dtype=jnp.int32)
    place = ((rows % 2) * 2 + rows // 2) * 32 + cols
    hit = (place[None, :] == jnp.arange(128, dtype=jnp.int32)[:, None]) & (ids < count)[None, :]
    table = jnp.concatenate([jnp.max(jnp.where(hit, ids[None, :], -1), axis=1), count])

    half = nodes // 2
    planes = (features, swap(features, "row", XL))
    held = [[planes[plane][part * half : (part + 1) * half]] for plane, part, _ in CHAINS]
    for step in range(4):
        for chain, (_, _, masks) in enumerate(CHAINS):
            so_far = held[chain][0] if step == 0 else jnp.concatenate(held[chain])
            held[chain] = [so_far, swap(so_far, "row", masks[step])]
        if step == 2:
            dense = make_dense(table, tiles.reshape(slots, tile, tile), *[parts[1] for parts in held])
    aggregate = 0.0
    for part in range(2):
        for chain in range(4):
            aggregate = aggregate + jnp.dot(
                dense[2 * chain + part], held[chain][part], preferred_element_type=F32
            )
    aggregate = aggregate.astype(BF)

    pair = aggregate[: 2 * nodes].astype(F32) + swap(aggregate[2 * nodes :], "col", CORE).astype(F32)
    aggregate = pair[:nodes] + swap(pair[nodes:].astype(BF), "col", XH).astype(F32)
    aggregate = aggregate.astype(BF)

    shifted = jnp.dot(aggregate, weight, preferred_element_type=F32) + bias[None, :]
    activations = jax.nn.silu(shifted).astype(BF)
    sig = jax.nn.sigmoid(shifted)
    slope = sig * (1.0 + shifted * (1.0 - sig))
    grad_pre = (cotangent.astype(F32) * slope).astype(BF)
    back = lax.dot_general(grad_pre, weight, (((1,), (1,)), ((), ())), preferred_element_type=F32).astype(BF)

    tie = zero_of(back)
    back = jnp.concatenate([back, swap(back, "col", XH)])
    back = jnp.concatenate([back, swap(back, "col", CORE)])
    back = lax.optimization_barrier(back)
    node_total = nodes * lax.axis_size("row") * lax.axis_size("col")
    quarter = lax.dot_general(aggregate, grad_pre, (((0,), (0,)), ((), ())), preferred_element_type=F32)
    quarter = halve(halve(quarter * node_total ** (-0.5) + tie, "col", CORE), "col", XH)
    quarter = both(quarter, "row", XL).astype(BF)

    def product(matrix):
        return lax.dot_general(matrix, back, (((0,), (0,)), ((), ())), preferred_element_type=F32).astype(BF)

    share = quarter.shape[0] // 2
    load = {0: quarter[:share], 1: quarter[share:], 2: None, 3: None}

    def send(value, chain, step):
        value = value.astype(BF)
        if load[chain] is None:
            return swap(value, "row", CHAINS[chain][2][step])
        got = swap(jnp.concatenate([value, load[chain]]), "row", CHAINS[chain][2][step])
        load[chain] = (load[chain].astype(F32) + got[-share:].astype(F32)).astype(BF)
        return got[:-share]

    got, near = {}, {}
    turn = (2, 3, 0, 1)
    for chain in turn:
        got[chain] = send(product(dense[2 * chain + 1]), chain, 3)
    for chain in turn:
        near[chain] = product(dense[2 * chain])
    for step in (2, 1, 0):
        for chain in turn:
            n = near[chain].shape[0] // 2
            there = near[chain][n:].astype(F32) + got[chain][n:].astype(F32)
            here = near[chain][:n].astype(F32) + got[chain][:n].astype(F32)
            near[chain] = here.astype(BF) if step else here
            got[chain] = send(there, chain, step)
    sums = {chain: near[chain] + got[chain].astype(F32) for chain in turn}
    other = jnp.concatenate([sums[2], sums[3]]).astype(BF)
    own = jnp.concatenate([sums[0], sums[1]])
    grad_features = (own + swap(other, "row", XL).astype(F32)).astype(BF)
    quarter = jnp.concatenate([load[0], load[1]])
    grad_weight = spread(spread(quarter, "col", XH), "col", CORE).astype(F32)
    return (activations, grad_features, grad_weight)


def solution(mesh):
    placed = (
        P(("col", "row"), None),
        P(),
        P(),
        P("row", "col", None, None, None),
        P("row", "col", None),
        P("row", "col", None),
        P("row", "col"),
        P(("row", "col"), None),
    )
    return jax.shard_map(
        on_device,
        mesh=mesh,
        in_specs=placed,
        out_specs=(P(("row", "col"), None), P(("col", "row"), None), P()),
        check_vma=False,
    )
```

```python
import jax
import jax.numpy as jnp
from jax import lax
from jax.experimental import pallas as pl
from jax.experimental.pallas import tpu as pltpu
from jax.sharding import PartitionSpec as P

BF = jnp.bfloat16
F32 = jnp.float32
XL = 4
CHAINS = ((0, 0, (1, 3, 8, 24)), (0, 1, (8, 24, 1, 3)), (1, 0, (3, 1, 24, 8)), (1, 1, (24, 8, 3, 1)))
CORE, XH = 1, 2


def swap(value, axis, mask):
    size = lax.axis_size(axis)
    return lax.ppermute(value, axis, [(i ^ mask, i) for i in range(size)])


def order_of(masks):
    order = [0]
    for mask in masks:
        order = order + [offset ^ mask for offset in order]
    return order


def dense_kernel(table, tiles, *refs):
    outs, (held, sems) = refs[-10:-2], refs[-2:]
    step = pl.program_id(0)
    tile = held.shape[-1]
    wide = tile // 2

    @pl.when(step == 0)
    def _():
        def start(slot, carry):
            pltpu.make_async_copy(tiles.at[slot], held.at[slot], sems.at[slot]).start()
            return carry

        lax.fori_loop(0, table[128], start, 0)

    for chain, (plane, half, masks) in enumerate(CHAINS):
        if half:
            continue
        for offset in order_of(masks):
            slot = table[step * 32 + (offset ^ (plane * XL))]
            spots = []
            for part in range(2):
                k = order_of(CHAINS[chain + part][2]).index(offset)
                spots.append((outs[2 * (chain + part) + k // 8], pl.ds((k % 8) * wide, wide)))

            @pl.when(slot >= 0)
            def _(slot=slot, spots=spots):
                pltpu.make_async_copy(tiles.at[slot], held.at[slot], sems.at[slot]).wait()
                for part, (out, lanes) in enumerate(spots):
                    out[:, lanes] = held[slot, :, part * wide : (part + 1) * wide]

            @pl.when(slot < 0)
            def _(spots=spots):
                for out, lanes in spots:
                    out[:, lanes] = jnp.zeros((tile, wide), out.dtype)


def make_dense(table, tiles, *after):
    slots, tile, _ = tiles.shape
    return pl.pallas_call(
        dense_kernel,
        grid=(4,),
        out_shape=(jax.ShapeDtypeStruct((4 * tile, 4 * tile), BF),) * 8,
        in_specs=[
            pl.BlockSpec(memory_space=pltpu.SMEM),
            pl.BlockSpec(memory_space=pl.ANY),
        ]
        + [pl.BlockSpec(memory_space=pl.ANY)] * len(after),
        out_specs=(pl.BlockSpec((tile, 4 * tile), lambda i: (i, 0)),) * 8,
        scratch_shapes=[pltpu.VMEM((slots, tile, tile), BF), pltpu.SemaphoreType.DMA((slots,))],
        compiler_params=pltpu.CompilerParams(vmem_limit_bytes=24 << 20),
        cost_estimate=pl.CostEstimate(flops=0, bytes_accessed=24 << 20, transcendentals=0),
    )(table, tiles, *after)


def zero_of(value):
    return value[0, 0].astype(F32) * 0.0


def pulse(*values):
    tiny = sum(value[:16, :128].astype(F32) for value in values).astype(BF)
    return zero_of(swap(tiny, "col", CORE))


def tied(value, zero):
    return lax.optimization_barrier((value.astype(F32) + zero).astype(BF))


def halve(value, axis, mask):
    half = value.shape[0] // 2
    bit = ((lax.axis_index(axis) & mask) != 0).astype(jnp.int32)
    value = value.astype(BF)
    mine = lax.dynamic_slice_in_dim(value, bit * half, half)
    other = lax.dynamic_slice_in_dim(value, (1 - bit) * half, half)
    return mine.astype(F32) + swap(other, axis, mask).astype(F32)


def both(value, axis, mask):
    value = value.astype(BF)
    return value.astype(F32) + swap(value, axis, mask).astype(F32)


def spread(value, axis, mask):
    value = value.astype(BF)
    other = swap(value, axis, mask)
    first = (lax.axis_index(axis) & mask) == 0
    return jnp.concatenate([jnp.where(first, value, other), jnp.where(first, other, value)])


def on_device(features, weight, bias, tiles, tile_rows, tile_cols, tile_count, cotangent):
    nodes, width = features.shape
    tile = tiles.shape[-1]
    slots = tiles.shape[2]
    row, col = lax.axis_index("row"), lax.axis_index("col")

    rows, cols = tile_rows.reshape(slots) ^ col, tile_cols.reshape(slots) ^ row
    count = tile_count.reshape(1)
    ids = jnp.arange(slots, dtype=jnp.int32)
    place = ((rows % 2) * 2 + rows // 2) * 32 + cols
    hit = (place[None, :] == jnp.arange(128, dtype=jnp.int32)[:, None]) & (ids < count)[None, :]
    table = jnp.concatenate([jnp.max(jnp.where(hit, ids[None, :], -1), axis=1), count])

    half = nodes // 2
    planes = (features, swap(features, "row", XL))
    held = [[planes[plane][part * half : (part + 1) * half]] for plane, part, _ in CHAINS]
    for step in range(4):
        for chain, (_, _, masks) in enumerate(CHAINS):
            so_far = held[chain][0] if step == 0 else jnp.concatenate(held[chain])
            held[chain] = [so_far, swap(so_far, "row", masks[step])]
        if step == 2:
            dense = make_dense(table, tiles.reshape(slots, tile, tile), *[parts[1] for parts in held])
    aggregate = 0.0
    for part in range(2):
        for chain in range(4):
            aggregate = aggregate + jnp.dot(
                dense[2 * chain + part], held[chain][part], preferred_element_type=F32
            )
    aggregate = aggregate.astype(BF)

    pair = aggregate[: 2 * nodes].astype(F32) + swap(aggregate[2 * nodes :], "col", CORE).astype(F32)
    aggregate = pair[:nodes] + swap(pair[nodes:].astype(BF), "col", XH).astype(F32)
    aggregate = aggregate.astype(BF)

    shifted = jnp.dot(aggregate, weight, preferred_element_type=F32) + bias[None, :]
    activations = jax.nn.silu(shifted).astype(BF)
    sig = jax.nn.sigmoid(shifted)
    slope = sig * (1.0 + shifted * (1.0 - sig))
    grad_pre = (cotangent.astype(F32) * slope).astype(BF)
    back = lax.dot_general(grad_pre, weight, (((1,), (1,)), ((), ())), preferred_element_type=F32).astype(BF)

    there = swap(back, "col", XH)
    tie = zero_of(there)
    back = jnp.concatenate([back, there])
    back = jnp.concatenate([back, swap(back, "col", CORE)])
    back = lax.optimization_barrier(back)
    node_total = nodes * lax.axis_size("row") * lax.axis_size("col")
    quarter = lax.dot_general(aggregate, grad_pre, (((0,), (0,)), ((), ())), preferred_element_type=F32)
    quarter = halve(halve(quarter * node_total ** (-0.5) + tie, "col", CORE), "col", XH)
    quarter = both(quarter, "row", XL).astype(BF)

    def product(matrix):
        return lax.dot_general(matrix, back, (((0,), (0,)), ((), ())), preferred_element_type=F32).astype(BF)

    share = quarter.shape[0] // 2
    load = {0: quarter[:share], 1: quarter[share:], 2: None, 3: None}

    def send(value, chain, step):
        value = value.astype(BF)
        if load[chain] is None:
            return swap(value, "row", CHAINS[chain][2][step])
        got = swap(jnp.concatenate([value, load[chain]]), "row", CHAINS[chain][2][step])
        load[chain] = (load[chain].astype(F32) + got[-share:].astype(F32)).astype(BF)
        return got[:-share]

    got, near = {}, {}
    turn = (2, 3, 0, 1)
    far = [product(dense[2 * chain + 1]) for chain in turn]
    for chain, value in zip(turn, far):
        got[chain] = send(value, chain, 3)
    back = tied(back, pulse(*far))
    for chain in turn:
        near[chain] = product(dense[2 * chain])
    for step in (2, 1, 0):
        for chain in turn:
            n = near[chain].shape[0] // 2
            there = near[chain][n:].astype(F32) + got[chain][n:].astype(F32)
            here = near[chain][:n].astype(F32) + got[chain][:n].astype(F32)
            near[chain] = here.astype(BF) if step else here
            got[chain] = send(there, chain, step)
    sums = {chain: near[chain] + got[chain].astype(F32) for chain in turn}
    other = jnp.concatenate([sums[2], sums[3]]).astype(BF)
    own = jnp.concatenate([sums[0], sums[1]])
    grad_features = (own + swap(other, "row", XL).astype(F32)).astype(BF)
    quarter = jnp.concatenate([load[0], load[1]])
    grad_weight = spread(spread(quarter, "col", XH), "col", CORE).astype(F32)
    return (activations, grad_features, grad_weight)


def solution(mesh):
    placed = (
        P(("col", "row"), None),
        P(),
        P(),
        P("row", "col", None, None, None),
        P("row", "col", None),
        P("row", "col", None),
        P("row", "col"),
        P(("row", "col"), None),
    )
    return jax.shard_map(
        on_device,
        mesh=mesh,
        in_specs=placed,
        out_specs=(P(("row", "col"), None), P(("col", "row"), None), P()),
        check_vma=False,
    )
```

```python
import jax
import jax.numpy as jnp
from jax import lax
from jax.experimental import pallas as pl
from jax.experimental.pallas import tpu as pltpu
from jax.sharding import PartitionSpec as P

BF = jnp.bfloat16
F32 = jnp.float32
XL = 4
CHAINS = ((0, 0, (1, 8, 3, 24)), (0, 1, (8, 1, 24, 3)), (1, 0, (3, 24, 1, 8)), (1, 1, (24, 3, 8, 1)))
CORE, XH = 1, 2


def swap(value, axis, mask):
    size = lax.axis_size(axis)
    return lax.ppermute(value, axis, [(i ^ mask, i) for i in range(size)])


def order_of(masks):
    order = [0]
    for mask in masks:
        order = order + [offset ^ mask for offset in order]
    return order


def dense_kernel(table, tiles, *refs):
    outs, (held, sems) = refs[-10:-2], refs[-2:]
    step = pl.program_id(0)
    tile = held.shape[-1]
    wide = tile // 2

    @pl.when(step == 0)
    def _():
        def start(slot, carry):
            pltpu.make_async_copy(tiles.at[slot], held.at[slot], sems.at[slot]).start()
            return carry

        lax.fori_loop(0, table[128], start, 0)

    for chain, (plane, half, masks) in enumerate(CHAINS):
        if half:
            continue
        for offset in order_of(masks):
            slot = table[step * 32 + (offset ^ (plane * XL))]
            spots = []
            for part in range(2):
                k = order_of(CHAINS[chain + part][2]).index(offset)
                spots.append((outs[2 * (chain + part) + k // 8], pl.ds((k % 8) * wide, wide)))

            @pl.when(slot >= 0)
            def _(slot=slot, spots=spots):
                pltpu.make_async_copy(tiles.at[slot], held.at[slot], sems.at[slot]).wait()
                for part, (out, lanes) in enumerate(spots):
                    out[:, lanes] = held[slot, :, part * wide : (part + 1) * wide]

            @pl.when(slot < 0)
            def _(spots=spots):
                for out, lanes in spots:
                    out[:, lanes] = jnp.zeros((tile, wide), out.dtype)


def make_dense(table, tiles, *after):
    slots, tile, _ = tiles.shape
    return pl.pallas_call(
        dense_kernel,
        grid=(4,),
        out_shape=(jax.ShapeDtypeStruct((4 * tile, 4 * tile), BF),) * 8,
        in_specs=[
            pl.BlockSpec(memory_space=pltpu.SMEM),
            pl.BlockSpec(memory_space=pl.ANY),
        ]
        + [pl.BlockSpec(memory_space=pl.ANY)] * len(after),
        out_specs=(pl.BlockSpec((tile, 4 * tile), lambda i: (i, 0)),) * 8,
        scratch_shapes=[pltpu.VMEM((slots, tile, tile), BF), pltpu.SemaphoreType.DMA((slots,))],
        compiler_params=pltpu.CompilerParams(vmem_limit_bytes=24 << 20),
        cost_estimate=pl.CostEstimate(flops=0, bytes_accessed=24 << 20, transcendentals=0),
    )(table, tiles, *after)


def zero_of(value):
    return value[0, 0].astype(F32) * 0.0


def pulse(*values):
    tiny = sum(value[:16, :128].astype(F32) for value in values).astype(BF)
    return zero_of(swap(tiny, "col", CORE))


def tied(value, zero):
    return lax.optimization_barrier((value.astype(F32) + zero).astype(BF))


def halve(value, axis, mask):
    half = value.shape[0] // 2
    bit = ((lax.axis_index(axis) & mask) != 0).astype(jnp.int32)
    value = value.astype(BF)
    mine = lax.dynamic_slice_in_dim(value, bit * half, half)
    other = lax.dynamic_slice_in_dim(value, (1 - bit) * half, half)
    return mine.astype(F32) + swap(other, axis, mask).astype(F32)


def both(value, axis, mask):
    value = value.astype(BF)
    return value.astype(F32) + swap(value, axis, mask).astype(F32)


def spread(value, axis, mask):
    value = value.astype(BF)
    other = swap(value, axis, mask)
    first = (lax.axis_index(axis) & mask) == 0
    return jnp.concatenate([jnp.where(first, value, other), jnp.where(first, other, value)])


def on_device(features, weight, bias, tiles, tile_rows, tile_cols, tile_count, cotangent):
    nodes, width = features.shape
    tile = tiles.shape[-1]
    slots = tiles.shape[2]
    row, col = lax.axis_index("row"), lax.axis_index("col")

    rows, cols = tile_rows.reshape(slots) ^ col, tile_cols.reshape(slots) ^ row
    count = tile_count.reshape(1)
    ids = jnp.arange(slots, dtype=jnp.int32)
    place = ((rows % 2) * 2 + rows // 2) * 32 + cols
    hit = (place[None, :] == jnp.arange(128, dtype=jnp.int32)[:, None]) & (ids < count)[None, :]
    table = jnp.concatenate([jnp.max(jnp.where(hit, ids[None, :], -1), axis=1), count])

    half = nodes // 2
    planes = (features, swap(features, "row", XL))
    held = [[planes[plane][part * half : (part + 1) * half]] for plane, part, _ in CHAINS]
    for step in range(4):
        for chain, (_, _, masks) in enumerate(CHAINS):
            so_far = held[chain][0] if step == 0 else jnp.concatenate(held[chain])
            held[chain] = [so_far, swap(so_far, "row", masks[step])]
        if step == 2:
            dense = make_dense(table, tiles.reshape(slots, tile, tile), *[parts[1] for parts in held])
    aggregate = 0.0
    for part in range(2):
        for chain in range(4):
            aggregate = aggregate + jnp.dot(
                dense[2 * chain + part], held[chain][part], preferred_element_type=F32
            )
    aggregate = aggregate.astype(BF)

    pair = aggregate[: 2 * nodes].astype(F32) + swap(aggregate[2 * nodes :], "col", CORE).astype(F32)
    aggregate = pair[:nodes] + swap(pair[nodes:].astype(BF), "col", XH).astype(F32)
    aggregate = aggregate.astype(BF)

    shifted = jnp.dot(aggregate, weight, preferred_element_type=F32) + bias[None, :]
    activations = jax.nn.silu(shifted).astype(BF)
    sig = jax.nn.sigmoid(shifted)
    slope = sig * (1.0 + shifted * (1.0 - sig))
    grad_pre = (cotangent.astype(F32) * slope).astype(BF)
    back = lax.dot_general(grad_pre, weight, (((1,), (1,)), ((), ())), preferred_element_type=F32).astype(BF)

    back = jnp.concatenate([back, swap(back, "col", XH)])
    back = jnp.concatenate([back, swap(back, "col", CORE)])
    back = lax.optimization_barrier(back)

    def product(matrix):
        return lax.dot_general(matrix, back, (((0,), (0,)), ((), ())), preferred_element_type=F32).astype(BF)

    share = width // 4
    load = {chain: None for chain in range(4)}

    def send(value, chain, step):
        value = value.astype(BF)
        if load[chain] is None:
            return swap(value, "row", CHAINS[chain][2][step])
        got = swap(jnp.concatenate([value, load[chain]]), "row", CHAINS[chain][2][step])
        load[chain] = (load[chain].astype(F32) + got[-share:].astype(F32)).astype(BF)
        return got[:-share]

    got, near = {}, {}
    turn = (2, 3, 0, 1)
    far = [product(dense[2 * chain + 1]) for chain in turn]
    for chain, value in zip(turn, far):
        got[chain] = send(value, chain, 3)
    tie = pulse(*far)
    back = tied(back, tie)
    for chain in turn:
        near[chain] = product(dense[2 * chain])

    node_total = nodes * lax.axis_size("row") * lax.axis_size("col")
    quarter = lax.dot_general(aggregate, grad_pre, (((0,), (0,)), ((), ())), preferred_element_type=F32)
    quarter = halve(halve(quarter * node_total ** (-0.5) + tie, "col", CORE), "col", XH)
    quarter = both(quarter, "row", XL)
    load[0] = both(quarter, "row", CHAINS[0][2][3]).astype(BF)
    for step in (2, 1, 0):
        for chain in turn:
            n = near[chain].shape[0] // 2
            there = near[chain][n:].astype(F32) + got[chain][n:].astype(F32)
            here = near[chain][:n].astype(F32) + got[chain][:n].astype(F32)
            near[chain] = here.astype(BF) if step else here
            got[chain] = send(there, chain, step)
    sums = {chain: near[chain] + got[chain].astype(F32) for chain in turn}
    other = jnp.concatenate([sums[2], sums[3]]).astype(BF)
    own = jnp.concatenate([sums[0], sums[1]])
    grad_features = (own + swap(other, "row", XL).astype(F32)).astype(BF)
    quarter = load[0]
    grad_weight = spread(spread(quarter, "col", XH), "col", CORE).astype(F32)
    return (activations, grad_features, grad_weight)


def solution(mesh):
    placed = (
        P(("col", "row"), None),
        P(),
        P(),
        P("row", "col", None, None, None),
        P("row", "col", None),
        P("row", "col", None),
        P("row", "col"),
        P(("row", "col"), None),
    )
    return jax.shard_map(
        on_device,
        mesh=mesh,
        in_specs=placed,
        out_specs=(P(("row", "col"), None), P(("col", "row"), None), P()),
        check_vma=False,
    )
```

```python
import jax
import jax.numpy as jnp
from jax import lax
from jax.experimental import pallas as pl
from jax.experimental.pallas import tpu as pltpu
from jax.sharding import PartitionSpec as P

BF = jnp.bfloat16
F32 = jnp.float32
XL = 4
CHAINS = ((0, 0, (1, 8, 3, 24)), (0, 1, (8, 1, 24, 3)), (1, 0, (3, 24, 1, 8)), (1, 1, (24, 3, 8, 1)))
CORE, XH = 1, 2


def swap(value, axis, mask):
    size = lax.axis_size(axis)
    return lax.ppermute(value, axis, [(i ^ mask, i) for i in range(size)])


def order_of(masks):
    order = [0]
    for mask in masks:
        order = order + [offset ^ mask for offset in order]
    return order


def dense_kernel(table, tiles, *refs):
    outs, (held, sems) = refs[-10:-2], refs[-2:]
    step = pl.program_id(0)
    tile = held.shape[-1]
    wide = tile // 2

    @pl.when(step == 0)
    def _():
        def start(slot, carry):
            pltpu.make_async_copy(tiles.at[slot], held.at[slot], sems.at[slot]).start()
            return carry

        lax.fori_loop(0, table[128], start, 0)

    for chain, (plane, half, masks) in enumerate(CHAINS):
        if half:
            continue
        for offset in order_of(masks):
            slot = table[step * 32 + (offset ^ (plane * XL))]
            spots = []
            for part in range(2):
                k = order_of(CHAINS[chain + part][2]).index(offset)
                spots.append((outs[2 * (chain + part) + k // 8], pl.ds((k % 8) * wide, wide)))

            @pl.when(slot >= 0)
            def _(slot=slot, spots=spots):
                pltpu.make_async_copy(tiles.at[slot], held.at[slot], sems.at[slot]).wait()
                for part, (out, lanes) in enumerate(spots):
                    out[:, lanes] = held[slot, :, part * wide : (part + 1) * wide]

            @pl.when(slot < 0)
            def _(spots=spots):
                for out, lanes in spots:
                    out[:, lanes] = jnp.zeros((tile, wide), out.dtype)


def make_dense(table, tiles, *after):
    slots, tile, _ = tiles.shape
    return pl.pallas_call(
        dense_kernel,
        grid=(4,),
        out_shape=(jax.ShapeDtypeStruct((4 * tile, 4 * tile), BF),) * 8,
        in_specs=[
            pl.BlockSpec(memory_space=pltpu.SMEM),
            pl.BlockSpec(memory_space=pl.ANY),
        ]
        + [pl.BlockSpec(memory_space=pl.ANY)] * len(after),
        out_specs=(pl.BlockSpec((tile, 4 * tile), lambda i: (i, 0)),) * 8,
        scratch_shapes=[pltpu.VMEM((slots, tile, tile), BF), pltpu.SemaphoreType.DMA((slots,))],
        compiler_params=pltpu.CompilerParams(vmem_limit_bytes=24 << 20),
        cost_estimate=pl.CostEstimate(flops=0, bytes_accessed=24 << 20, transcendentals=0),
    )(table, tiles, *after)


def zero_of(value):
    return value[0, 0].astype(F32) * 0.0


def pulse(*values):
    tiny = sum(value[:16, :128].astype(F32) for value in values).astype(BF)
    return zero_of(swap(tiny, "col", CORE))


def tied(value, zero):
    return lax.optimization_barrier((value.astype(F32) + zero).astype(BF))


def halve(value, axis, mask):
    half = value.shape[0] // 2
    bit = ((lax.axis_index(axis) & mask) != 0).astype(jnp.int32)
    value = value.astype(BF)
    mine = lax.dynamic_slice_in_dim(value, bit * half, half)
    other = lax.dynamic_slice_in_dim(value, (1 - bit) * half, half)
    return mine.astype(F32) + swap(other, axis, mask).astype(F32)


def both(value, axis, mask):
    value = value.astype(BF)
    return value.astype(F32) + swap(value, axis, mask).astype(F32)


def spread(value, axis, mask):
    value = value.astype(BF)
    other = swap(value, axis, mask)
    first = (lax.axis_index(axis) & mask) == 0
    return jnp.concatenate([jnp.where(first, value, other), jnp.where(first, other, value)])


def on_device(features, weight, bias, tiles, tile_rows, tile_cols, tile_count, cotangent):
    nodes, width = features.shape
    tile = tiles.shape[-1]
    slots = tiles.shape[2]
    row, col = lax.axis_index("row"), lax.axis_index("col")

    rows, cols = tile_rows.reshape(slots) ^ col, tile_cols.reshape(slots) ^ row
    count = tile_count.reshape(1)
    ids = jnp.arange(slots, dtype=jnp.int32)
    place = ((rows % 2) * 2 + rows // 2) * 32 + cols
    hit = (place[None, :] == jnp.arange(128, dtype=jnp.int32)[:, None]) & (ids < count)[None, :]
    table = jnp.concatenate([jnp.max(jnp.where(hit, ids[None, :], -1), axis=1), count])

    half = nodes // 2
    planes = (features, swap(features, "row", XL))
    held = [[planes[plane][part * half : (part + 1) * half]] for plane, part, _ in CHAINS]
    for step in range(4):
        for chain, (_, _, masks) in enumerate(CHAINS):
            so_far = held[chain][0] if step == 0 else jnp.concatenate(held[chain])
            held[chain] = [so_far, swap(so_far, "row", masks[step])]
        if step == 2:
            there = swap(cotangent, "col", XH)
            dense = make_dense(table, tiles.reshape(slots, tile, tile), there, *[parts[1] for parts in held])
            cotangents = jnp.concatenate([cotangent, there])
    aggregate = 0.0
    for part in range(2):
        for chain in range(4):
            aggregate = aggregate + jnp.dot(
                dense[2 * chain + part], held[chain][part], preferred_element_type=F32
            )
    aggregate = aggregate.astype(BF)

    pair = aggregate[: 2 * nodes].astype(F32) + swap(aggregate[2 * nodes :], "col", CORE).astype(F32)
    pair = pair.astype(BF)
    there = swap(pair, "col", XH).astype(F32)
    aggregate = pair.astype(F32) + jnp.concatenate([there[nodes:], there[:nodes]])
    aggregate = aggregate.astype(BF)

    shifted = jnp.dot(aggregate, weight, preferred_element_type=F32) + bias[None, :]
    sig = jax.nn.sigmoid(shifted)
    activations = (shifted[:nodes] * sig[:nodes]).astype(BF)
    slope = sig * (1.0 + shifted * (1.0 - sig))
    grad_pre = (cotangents.astype(F32) * slope).astype(BF)
    back = lax.dot_general(grad_pre, weight, (((1,), (1,)), ((), ())), preferred_element_type=F32).astype(BF)

    back = jnp.concatenate([back, swap(back, "col", CORE)])
    back = lax.optimization_barrier(back)

    def product(matrix):
        return lax.dot_general(matrix, back, (((0,), (0,)), ((), ())), preferred_element_type=F32).astype(BF)

    share = width // 4
    load = {chain: None for chain in range(4)}

    def send(value, chain, step):
        value = value.astype(BF)
        if load[chain] is None:
            return swap(value, "row", CHAINS[chain][2][step])
        got = swap(jnp.concatenate([value, load[chain]]), "row", CHAINS[chain][2][step])
        load[chain] = (load[chain].astype(F32) + got[-share:].astype(F32)).astype(BF)
        return got[:-share]

    got, near = {}, {}
    turn = (2, 3, 0, 1)
    far = [product(dense[2 * chain + 1]) for chain in turn]
    for chain, value in zip(turn, far):
        got[chain] = send(value, chain, 3)
    tie = pulse(*far)
    back = tied(back, tie)
    for chain in turn:
        near[chain] = product(dense[2 * chain])

    node_total = nodes * lax.axis_size("row") * lax.axis_size("col")
    quarter = lax.dot_general(aggregate, grad_pre, (((0,), (0,)), ((), ())), preferred_element_type=F32)
    quarter = halve(quarter * node_total ** (-0.5) + tie, "col", CORE)
    quarter = lax.dynamic_slice_in_dim(quarter, (col // 2) * share, share)
    quarter = both(quarter, "row", XL)
    load[2] = both(quarter, "row", CHAINS[2][2][3]).astype(BF)
    for step in (2, 1, 0):
        for chain in turn:
            n = near[chain].shape[0] // 2
            there = near[chain][n:].astype(F32) + got[chain][n:].astype(F32)
            here = near[chain][:n].astype(F32) + got[chain][:n].astype(F32)
            near[chain] = here.astype(BF) if step else here
            got[chain] = send(there, chain, step)
    sums = {chain: near[chain] + got[chain].astype(F32) for chain in turn}
    other = jnp.concatenate([sums[2], sums[3]]).astype(BF)
    own = jnp.concatenate([sums[0], sums[1]])
    grad_features = (own + swap(other, "row", XL).astype(F32)).astype(BF)
    quarter = load[2]
    grad_weight = spread(spread(quarter, "col", XH), "col", CORE).astype(F32)
    return (activations, grad_features, grad_weight)


def solution(mesh):
    placed = (
        P(("col", "row"), None),
        P(),
        P(),
        P("row", "col", None, None, None),
        P("row", "col", None),
        P("row", "col", None),
        P("row", "col"),
        P(("row", "col"), None),
    )
    return jax.shard_map(
        on_device,
        mesh=mesh,
        in_specs=placed,
        out_specs=(P(("row", "col"), None), P(("col", "row"), None), P()),
        check_vma=False,
    )
```

```python
import jax
import jax.numpy as jnp
from jax import lax
from jax.experimental import pallas as pl
from jax.experimental.pallas import tpu as pltpu
from jax.sharding import PartitionSpec as P

BF = jnp.bfloat16
F32 = jnp.float32
XL = 4
CHAINS = ((0, 0, (1, 8, 3, 24)), (0, 1, (8, 1, 24, 3)), (1, 0, (3, 24, 1, 8)), (1, 1, (24, 3, 8, 1)))
CORE, XH = 1, 2


def swap(value, axis, mask):
    size = lax.axis_size(axis)
    return lax.ppermute(value, axis, [(i ^ mask, i) for i in range(size)])


def order_of(masks):
    order = [0]
    for mask in masks:
        order = order + [offset ^ mask for offset in order]
    return order


def dense_kernel(table, tiles, *refs):
    outs, (held, sems) = refs[-10:-2], refs[-2:]
    step = pl.program_id(0)
    tile = held.shape[-1]
    wide = tile // 2

    @pl.when(step == 0)
    def _():
        def start(slot, carry):
            pltpu.make_async_copy(tiles.at[slot], held.at[slot], sems.at[slot]).start()
            return carry

        lax.fori_loop(0, table[128], start, 0)

    for chain, (plane, half, masks) in enumerate(CHAINS):
        if half:
            continue
        for offset in order_of(masks):
            slot = table[step * 32 + (offset ^ (plane * XL))]
            spots = []
            for part in range(2):
                k = order_of(CHAINS[chain + part][2]).index(offset)
                spots.append((outs[2 * (chain + part) + k // 8], pl.ds((k % 8) * wide, wide)))

            @pl.when(slot >= 0)
            def _(slot=slot, spots=spots):
                pltpu.make_async_copy(tiles.at[slot], held.at[slot], sems.at[slot]).wait()
                for part, (out, lanes) in enumerate(spots):
                    out[:, lanes] = held[slot, :, part * wide : (part + 1) * wide]

            @pl.when(slot < 0)
            def _(spots=spots):
                for out, lanes in spots:
                    out[:, lanes] = jnp.zeros((tile, wide), out.dtype)


def make_dense(table, tiles, *after):
    slots, tile, _ = tiles.shape
    return pl.pallas_call(
        dense_kernel,
        grid=(4,),
        out_shape=(jax.ShapeDtypeStruct((4 * tile, 4 * tile), BF),) * 8,
        in_specs=[
            pl.BlockSpec(memory_space=pltpu.SMEM),
            pl.BlockSpec(memory_space=pl.ANY),
        ]
        + [pl.BlockSpec(memory_space=pl.ANY)] * len(after),
        out_specs=(pl.BlockSpec((tile, 4 * tile), lambda i: (i, 0)),) * 8,
        scratch_shapes=[pltpu.VMEM((slots, tile, tile), BF), pltpu.SemaphoreType.DMA((slots,))],
        compiler_params=pltpu.CompilerParams(vmem_limit_bytes=24 << 20),
        cost_estimate=pl.CostEstimate(flops=0, bytes_accessed=24 << 20, transcendentals=0),
    )(table, tiles, *after)


def zero_of(value):
    return value[0, 0].astype(F32) * 0.0


def pulse(*values):
    tiny = sum(value[:16, :128].astype(F32) for value in values).astype(BF)
    return zero_of(swap(tiny, "col", CORE))


def tied(value, zero):
    return lax.optimization_barrier((value.astype(F32) + zero).astype(BF))


def halve(value, axis, mask):
    half = value.shape[0] // 2
    bit = ((lax.axis_index(axis) & mask) != 0).astype(jnp.int32)
    value = value.astype(BF)
    mine = lax.dynamic_slice_in_dim(value, bit * half, half)
    other = lax.dynamic_slice_in_dim(value, (1 - bit) * half, half)
    return mine.astype(F32) + swap(other, axis, mask).astype(F32)


def both(value, axis, mask):
    value = value.astype(BF)
    return value.astype(F32) + swap(value, axis, mask).astype(F32)


def spread(value, axis, mask):
    value = value.astype(BF)
    other = swap(value, axis, mask)
    first = (lax.axis_index(axis) & mask) == 0
    return jnp.concatenate([jnp.where(first, value, other), jnp.where(first, other, value)])


def on_device(features, weight, bias, tiles, tile_rows, tile_cols, tile_count, cotangent):
    nodes, width = features.shape
    tile = tiles.shape[-1]
    slots = tiles.shape[2]
    row, col = lax.axis_index("row"), lax.axis_index("col")

    rows, cols = tile_rows.reshape(slots) ^ col, tile_cols.reshape(slots) ^ row
    count = tile_count.reshape(1)
    ids = jnp.arange(slots, dtype=jnp.int32)
    place = ((rows % 2) * 2 + rows // 2) * 32 + cols
    hit = (place[None, :] == jnp.arange(128, dtype=jnp.int32)[:, None]) & (ids < count)[None, :]
    table = jnp.concatenate([jnp.max(jnp.where(hit, ids[None, :], -1), axis=1), count])

    half = nodes // 2
    planes = (features, swap(features, "row", XL))
    held = [[planes[plane][part * half : (part + 1) * half]] for plane, part, _ in CHAINS]
    for step in range(4):
        for chain, (_, _, masks) in enumerate(CHAINS):
            so_far = held[chain][0] if step == 0 else jnp.concatenate(held[chain])
            held[chain] = [so_far, swap(so_far, "row", masks[step])]
        if step == 2:
            there = swap(cotangent, "col", XH)
            dense = make_dense(table, tiles.reshape(slots, tile, tile), there, *[parts[1] for parts in held])
            cotangents = jnp.concatenate([cotangent, there])
    aggregate = 0.0
    for part in range(2):
        for chain in range(4):
            aggregate = aggregate + jnp.dot(
                dense[2 * chain + part], held[chain][part], preferred_element_type=F32
            )
    aggregate = aggregate.astype(BF)

    pair = aggregate[: 2 * nodes].astype(F32) + swap(aggregate[2 * nodes :], "col", CORE).astype(F32)
    pair = pair.astype(BF)
    there = swap(pair, "col", XH).astype(F32)
    aggregate = pair.astype(F32) + jnp.concatenate([there[nodes:], there[:nodes]])
    aggregate = aggregate.astype(BF)

    shifted = jnp.dot(aggregate, weight, preferred_element_type=F32) + bias[None, :]
    sig = jax.nn.sigmoid(shifted)
    activations = (shifted[:nodes] * sig[:nodes]).astype(BF)
    slope = sig * (1.0 + shifted * (1.0 - sig))
    grad_pre = (cotangents.astype(F32) * slope).astype(BF)
    back = lax.dot_general(grad_pre, weight, (((1,), (1,)), ((), ())), preferred_element_type=F32).astype(BF)

    back = jnp.concatenate([back, swap(back, "col", CORE)])
    back = lax.optimization_barrier(back)

    def product(matrix):
        return lax.dot_general(matrix, back, (((0,), (0,)), ((), ())), preferred_element_type=F32).astype(BF)

    share = width // 4
    load = {chain: None for chain in range(4)}

    def send(value, chain, step):
        value = value.astype(BF)
        if load[chain] is None:
            return swap(value, "row", CHAINS[chain][2][step])
        got = swap(jnp.concatenate([value, load[chain]]), "row", CHAINS[chain][2][step])
        load[chain] = (load[chain].astype(F32) + got[-share:].astype(F32)).astype(BF)
        return got[:-share]

    got, near = {}, {}
    turn = (2, 3, 0, 1)
    far = [product(dense[2 * chain + 1]) for chain in turn]
    for chain, value in zip(turn, far):
        got[chain] = send(value, chain, 3)
    tie = pulse(*far)
    back = tied(back, tie)
    for chain in turn:
        near[chain] = product(dense[2 * chain])

    node_total = nodes * lax.axis_size("row") * lax.axis_size("col")
    quarter = lax.dot_general(aggregate, grad_pre, (((0,), (0,)), ((), ())), preferred_element_type=F32)
    quarter = halve(quarter * node_total ** (-0.5) + tie, "col", CORE)
    quarter = lax.dynamic_slice_in_dim(quarter, (col // 2) * share, share)
    quarter = both(quarter, "row", XL)
    load[2] = both(quarter, "row", CHAINS[2][2][3]).astype(BF)
    for step in (2, 1, 0):
        for chain in turn:
            n = near[chain].shape[0] // 2
            there = near[chain][n:].astype(F32) + got[chain][n:].astype(F32)
            here = near[chain][:n].astype(F32) + got[chain][:n].astype(F32)
            near[chain] = here.astype(BF) if step else here
            got[chain] = send(there, chain, step)
    sums = {chain: near[chain] + got[chain].astype(F32) for chain in turn}
    own = [sums[chain] + swap(sums[chain + 2].astype(BF), "row", XL).astype(F32) for chain in range(2)]
    grad_features = jnp.concatenate(own).astype(BF)
    quarter = load[2]
    grad_weight = spread(spread(quarter, "col", XH), "col", CORE).astype(F32)
    return (activations, grad_features, grad_weight)


def solution(mesh):
    placed = (
        P(("col", "row"), None),
        P(),
        P(),
        P("row", "col", None, None, None),
        P("row", "col", None),
        P("row", "col", None),
        P("row", "col"),
        P(("row", "col"), None),
    )
    return jax.shard_map(
        on_device,
        mesh=mesh,
        in_specs=placed,
        out_specs=(P(("row", "col"), None), P(("col", "row"), None), P()),
        check_vma=False,
    )
```

```python
import jax
import jax.numpy as jnp
from jax import lax
from jax.experimental import pallas as pl
from jax.experimental.pallas import tpu as pltpu
from jax.sharding import PartitionSpec as P

BF = jnp.bfloat16
F32 = jnp.float32
XL = 4
CHAINS = ((0, 0, (1, 8, 3, 24)), (0, 1, (8, 1, 24, 3)), (1, 0, (3, 24, 1, 8)), (1, 1, (24, 3, 8, 1)))
CORE, XH = 1, 2


def swap(value, axis, mask):
    size = lax.axis_size(axis)
    return lax.ppermute(value, axis, [(i ^ mask, i) for i in range(size)])


def order_of(masks):
    order = [0]
    for mask in masks:
        order = order + [offset ^ mask for offset in order]
    return order


def dense_kernel(table, tiles, *refs):
    outs, (held, sems) = refs[-10:-2], refs[-2:]
    step = pl.program_id(0)
    tile = held.shape[-1]
    wide = tile // 2

    @pl.when(step == 0)
    def _():
        def start(slot, carry):
            pltpu.make_async_copy(tiles.at[slot], held.at[slot], sems.at[slot]).start()
            return carry

        lax.fori_loop(0, table[128], start, 0)

    for chain, (plane, half, masks) in enumerate(CHAINS):
        if half:
            continue
        for offset in order_of(masks):
            slot = table[step * 32 + (offset ^ (plane * XL))]
            spots = []
            for part in range(2):
                k = order_of(CHAINS[chain + part][2]).index(offset)
                spots.append((outs[2 * (chain + part) + k // 8], pl.ds((k % 8) * wide, wide)))

            @pl.when(slot >= 0)
            def _(slot=slot, spots=spots):
                pltpu.make_async_copy(tiles.at[slot], held.at[slot], sems.at[slot]).wait()
                for part, (out, lanes) in enumerate(spots):
                    out[:, lanes] = held[slot, :, part * wide : (part + 1) * wide]

            @pl.when(slot < 0)
            def _(spots=spots):
                for out, lanes in spots:
                    out[:, lanes] = jnp.zeros((tile, wide), out.dtype)


def make_dense(table, tiles, *after):
    slots, tile, _ = tiles.shape
    return pl.pallas_call(
        dense_kernel,
        grid=(4,),
        out_shape=(jax.ShapeDtypeStruct((4 * tile, 4 * tile), BF),) * 8,
        in_specs=[
            pl.BlockSpec(memory_space=pltpu.SMEM),
            pl.BlockSpec(memory_space=pl.ANY),
        ]
        + [pl.BlockSpec(memory_space=pl.ANY)] * len(after),
        out_specs=(pl.BlockSpec((tile, 4 * tile), lambda i: (i, 0)),) * 8,
        scratch_shapes=[pltpu.VMEM((slots, tile, tile), BF), pltpu.SemaphoreType.DMA((slots,))],
        compiler_params=pltpu.CompilerParams(vmem_limit_bytes=24 << 20),
        cost_estimate=pl.CostEstimate(flops=0, bytes_accessed=24 << 20, transcendentals=0),
    )(table, tiles, *after)


def zero_of(value):
    return value[0, 0].astype(F32) * 0.0


def pulse(*values):
    tiny = sum(value[:16, :128].astype(F32) for value in values).astype(BF)
    return zero_of(swap(tiny, "col", CORE))


def tied(value, zero):
    return lax.optimization_barrier((value.astype(F32) + zero).astype(BF))


def halve(value, axis, mask):
    half = value.shape[0] // 2
    bit = ((lax.axis_index(axis) & mask) != 0).astype(jnp.int32)
    value = value.astype(BF)
    mine = lax.dynamic_slice_in_dim(value, bit * half, half)
    other = lax.dynamic_slice_in_dim(value, (1 - bit) * half, half)
    return mine.astype(F32) + swap(other, axis, mask).astype(F32)


def both(value, axis, mask):
    value = value.astype(BF)
    return value.astype(F32) + swap(value, axis, mask).astype(F32)


def spread(value, axis, mask):
    value = value.astype(BF)
    other = swap(value, axis, mask)
    first = (lax.axis_index(axis) & mask) == 0
    return jnp.concatenate([jnp.where(first, value, other), jnp.where(first, other, value)])


def on_device(features, weight, bias, tiles, tile_rows, tile_cols, tile_count, cotangent):
    nodes, width = features.shape
    tile = tiles.shape[-1]
    slots = tiles.shape[2]
    row, col = lax.axis_index("row"), lax.axis_index("col")

    rows, cols = tile_rows.reshape(slots) ^ col, tile_cols.reshape(slots) ^ row
    count = tile_count.reshape(1)
    ids = jnp.arange(slots, dtype=jnp.int32)
    place = ((rows % 2) * 2 + rows // 2) * 32 + cols
    hit = (place[None, :] == jnp.arange(128, dtype=jnp.int32)[:, None]) & (ids < count)[None, :]
    table = jnp.concatenate([jnp.max(jnp.where(hit, ids[None, :], -1), axis=1), count])

    half = nodes // 2
    planes = (features, swap(features, "row", XL))
    held = [[planes[plane][part * half : (part + 1) * half]] for plane, part, _ in CHAINS]
    for step in range(4):
        for chain, (_, _, masks) in enumerate(CHAINS):
            so_far = held[chain][0] if step == 0 else jnp.concatenate(held[chain])
            held[chain] = [so_far, swap(so_far, "row", masks[step])]
        if step == 2:
            there = swap(cotangent, "col", XH)
            dense = make_dense(table, tiles.reshape(slots, tile, tile), there, *[parts[1] for parts in held])
            cotangents = jnp.concatenate([cotangent, there])
    aggregate = 0.0
    for part in range(2):
        for chain in range(4):
            aggregate = aggregate + jnp.dot(
                dense[2 * chain + part], held[chain][part], preferred_element_type=F32
            )
    aggregate = aggregate.astype(BF)

    pair = aggregate[: 2 * nodes].astype(F32) + swap(aggregate[2 * nodes :], "col", CORE).astype(F32)
    pair = pair.astype(BF)
    there = swap(pair, "col", XH).astype(F32)
    aggregate = pair.astype(F32) + jnp.concatenate([there[nodes:], there[:nodes]])
    aggregate = aggregate.astype(BF)

    shifted = jnp.dot(aggregate, weight, preferred_element_type=F32) + bias[None, :]
    sig = jax.nn.sigmoid(shifted)
    activations = (shifted[:nodes] * sig[:nodes]).astype(BF)
    slope = sig * (1.0 + shifted * (1.0 - sig))
    grad_pre = (cotangents.astype(F32) * slope).astype(BF)
    back = lax.dot_general(grad_pre, weight, (((1,), (1,)), ((), ())), preferred_element_type=F32).astype(BF)

    back = jnp.concatenate([back, swap(back, "col", CORE)])
    back = lax.optimization_barrier(back)

    def product(matrix):
        return lax.dot_general(matrix, back, (((0,), (0,)), ((), ())), preferred_element_type=F32).astype(BF)

    share = width // 4
    load = {chain: None for chain in range(4)}

    def send(value, chain, step):
        value = value.astype(BF)
        if load[chain] is None:
            return swap(value, "row", CHAINS[chain][2][step])
        got = swap(jnp.concatenate([value, load[chain]]), "row", CHAINS[chain][2][step])
        load[chain] = (load[chain].astype(F32) + got[-share:].astype(F32)).astype(BF)
        return got[:-share]

    got, near = {}, {}
    turn = (2, 3, 0, 1)
    far = [product(dense[2 * chain + 1]) for chain in turn]
    for chain, value in zip(turn, far):
        got[chain] = send(value, chain, 3)
    tie = pulse(far[-1])
    back = tied(back, tie)
    for chain in turn:
        near[chain] = product(dense[2 * chain])

    node_total = nodes * lax.axis_size("row") * lax.axis_size("col")
    quarter = lax.dot_general(aggregate, grad_pre, (((0,), (0,)), ((), ())), preferred_element_type=F32)
    quarter = halve(quarter * node_total ** (-0.5) + tie, "col", CORE)
    quarter = lax.dynamic_slice_in_dim(quarter, (col // 2) * share, share)
    quarter = both(quarter, "row", XL)
    load[2] = both(quarter, "row", CHAINS[2][2][3]).astype(BF)
    for step in (2, 1, 0):
        for chain in turn:
            n = near[chain].shape[0] // 2
            there = near[chain][n:].astype(F32) + got[chain][n:].astype(F32)
            here = near[chain][:n].astype(F32) + got[chain][:n].astype(F32)
            near[chain] = here.astype(BF) if step else here
            got[chain] = send(there, chain, step)
    sums = {chain: near[chain] + got[chain].astype(F32) for chain in turn}
    own = [sums[chain] + swap(sums[chain + 2].astype(BF), "row", XL).astype(F32) for chain in range(2)]
    grad_features = jnp.concatenate(own).astype(BF)
    quarter = load[2]
    grad_weight = spread(spread(quarter, "col", XH), "col", CORE).astype(F32)
    return (activations, grad_features, grad_weight)


def solution(mesh):
    placed = (
        P(("col", "row"), None),
        P(),
        P(),
        P("row", "col", None, None, None),
        P("row", "col", None),
        P("row", "col", None),
        P("row", "col"),
        P(("row", "col"), None),
    )
    return jax.shard_map(
        on_device,
        mesh=mesh,
        in_specs=placed,
        out_specs=(P(("row", "col"), None), P(("col", "row"), None), P()),
        check_vma=False,
    )
```
